256 devices in a mesh: pool: 32 (over y, x, z_hi), tp: 8 (over z_lo, core).
Axes of the slice: x: 4, y: 4, z: 8 (z_hi: 2, z_lo: 4; z = z_hi * 4 + z_lo), core: 2. Of those that a mesh axis runs over, the one named last changes fastest.
Arguments:
- queries: bfloat16 [2, 4096, 8192], P(None, 'pool', 'tp'), may hold values from -24 to 24
- new_kv: bfloat16 [2, 8, 2, 4096, 128], P(None, 'tp', None, 'pool'), may hold values from -6 to 6
- kv_pool: bfloat16 [96, 8, 2, 128, 128], P('pool', 'tp'), may hold values from -6 to 6
- block_owner: int32 [2, 48], replicated, may hold values from 0 to 31, as said below
- block_slot: int32 [2, 48], replicated, may hold values from 0 to 2
- prefix_len: int32 [2], replicated, may hold values from 1921 to 6144, as said below
- decode_page: int32 [2, 32], replicated, may hold values from 0 to 63, as said below
- out_weight: bfloat16 [8192, 4096], P('tp'), may hold values from -1 to 1
Outputs:
- attn_out: bfloat16 [2, 4096, 4096], P(None, 'pool', 'tp')
- decode_cache: bfloat16 [64, 8, 2, 128, 128], P('pool', 'tp')
The draws below stay inside these ranges and needn't reach their ends.
Inputs may be any that keep to these rules, and one draw needn't show every extreme that they name: block_owner[r, j] and block_slot[r, j] together name row block_owner[r, j] * 3 + block_slot[r, j] of kv_pool, and every row of kv_pool is named exactly once. Of the rows named by entries j with j * 128 < prefix_len[r], every pool device holds exactly 2. `prefix_len`: one request's prefix is 6144 tokens long. `decode_page`: each of the 64 decode pages is named exactly once.
All inputs are finite; a program needn't handle non-finite values.
Results may differ from the reference program's by a relative error of at most 0.02.
Values may be sent and summed in bfloat16 or wider, within the bound.
A program may use at most 64 MiB of HBM per device.

```python
import math
import jax
import jax.numpy as jnp
from jax import lax

HEADS = 64
KV_HEADS = 8
HD = 128
OUT_W = 4096
PAGE = 128
REQS = 2
POOL_DEV = 3
LIVE_DEV = 2
GROUP = 8
MAXBLK = 48
NEW = 4096
NEWP = 32
DEC_PAGES = 64
N_POOL = 32


def page_tables(key):
    part_keys = jax.random.split(key, 6)
    owners = MAXBLK * REQS // POOL_DEV
    full_request = jax.random.randint(part_keys[0], (), 0, REQS)
    request_ids = jnp.arange(REQS)
    rest_blocks = owners * LIVE_DEV - MAXBLK
    block_count = jnp.where(request_ids == full_request, MAXBLK, rest_blocks)
    tail_len = jax.random.randint(part_keys[1], (REQS,), 1, PAGE + 1)
    prefix_tokens = (block_count - 1) * PAGE + jnp.where(request_ids == full_request, PAGE, tail_len)
    round_keys = jax.random.split(part_keys[2], POOL_DEV)
    round_order = jax.vmap(lambda one_key: jax.random.permutation(one_key, owners))(round_keys)
    slot_keys = jax.random.split(part_keys[3], owners)
    slot_order = jax.vmap(lambda one_key: jax.random.permutation(one_key, POOL_DEV))(slot_keys)
    seq_owner = round_order.reshape(-1)
    seq_round = jnp.repeat(jnp.arange(POOL_DEV), owners)
    seq_slot = slot_order[seq_owner, seq_round]
    live_total = owners * LIVE_DEV
    live_shuffle = jax.random.permutation(part_keys[4], live_total)
    dead_shuffle = jax.random.permutation(part_keys[5], owners * POOL_DEV - live_total)
    order_all = jnp.concatenate([live_shuffle, live_total + dead_shuffle])
    entry_live = (jnp.arange(MAXBLK)[None, :] < block_count[:, None]).reshape(-1).astype(jnp.int32)
    live_rank = jnp.cumsum(entry_live) - 1
    dead_rank = jnp.cumsum(1 - entry_live) - 1
    position = jnp.where(entry_live == 1, live_rank, live_total + dead_rank)
    source = order_all[position]
    owner_ids = seq_owner[source].reshape(REQS, MAXBLK).astype(jnp.int32)
    slot_ids = seq_slot[source].reshape(REQS, MAXBLK).astype(jnp.int32)
    return (owner_ids, slot_ids, prefix_tokens.astype(jnp.int32))


def draw_block_owner(key, part):
    owner_ids, slot_ids, prefix_tokens = page_tables(key)
    return owner_ids


def draw_block_slot(key, part):
    owner_ids, slot_ids, prefix_tokens = page_tables(key)
    return slot_ids


def draw_prefix_len(key, part):
    owner_ids, slot_ids, prefix_tokens = page_tables(key)
    return prefix_tokens


def draw_decode_page(key, part):
    key = jax.random.fold_in(key, 7)
    order_all = jax.random.permutation(key, DEC_PAGES)
    return order_all.reshape(REQS, NEWP).astype(jnp.int32)


def draw_new_kv(key, part):
    key = jax.random.fold_in(key, 3)
    shape_all = (REQS, KV_HEADS, 2, NEW, HD)
    result = jnp.clip(jax.random.normal(key, shape_all, jnp.float32), -6.0, 6.0)
    return result.astype(jnp.bfloat16)


def draw_queries(key, part):
    key = jax.random.fold_in(key, 5)
    result = jnp.clip(2.0 * jax.random.normal(key, (REQS, NEW, HEADS * HD), jnp.float32), -12.0, 12.0)
    return result.astype(jnp.bfloat16)


def raised(values, rng, source, target, shards_of, factor):
    owner, partner = [(jnp.arange(values.shape[dim]) // (values.shape[dim] // shards_of)).reshape([-1 if axis == dim else 1 for axis in range(values.ndim)]) for dim in (source, target)]
    chosen = jax.random.permutation(rng, shards_of)[partner]
    strong = (owner == chosen) | (owner == (partner + shards_of // 2) % shards_of)
    return jnp.where(strong, factor * values, values)


def steps_of(own_key, dims, cuts, smallest, high):
    factor_of = 1.0
    for axis_at, shards_of in cuts:
        draws = jax.random.uniform(jax.random.fold_in(jax.random.fold_in(own_key, 6), axis_at), (shards_of,), jnp.float32, smallest / len(cuts), high / len(cuts))
        factor_of = factor_of * jnp.repeat(jnp.exp(draws), dims[axis_at] // shards_of).reshape((-1,) + (1,) * (len(dims) - 1 - axis_at))
    return factor_of


def bell_draw(rng, dims, scale, reach, pieces=(), held_as=jnp.bfloat16):
    values = scale * jax.random.normal(rng, dims, jnp.float32)
    if pieces:
        values = values * steps_of(rng, dims, pieces, -0.22, 0.18)
    return jnp.clip(values, -reach, reach).astype(held_as)


def noise_with(own_key, shape, scale, limit, cuts, heavy, kind=jnp.bfloat16):
    drawn = scale * jax.random.normal(own_key, shape, jnp.float32)
    if cuts:
        drawn = drawn * steps_of(own_key, shape, cuts, -0.22, 0.18)
    return jnp.clip(raised(drawn, jax.random.fold_in(own_key, 3), *heavy), -limit, limit).astype(kind)


def setup_inputs(seed: int = 0) -> dict:
    seeds = jax.random.split(jax.random.key(seed), 9)
    queries = draw_queries(jax.random.fold_in(seeds[8], 71), 0)
    new_kv = draw_new_kv(jax.random.fold_in(seeds[8], 71), 0)
    kv_pool = bell_draw(seeds[2], (N_POOL * POOL_DEV, KV_HEADS, 2, PAGE, HD), 1.0, 6.0, ((0, 32), (1, 8)))
    block_owner = draw_block_owner(jax.random.fold_in(seeds[8], 71), 0)
    block_slot = draw_block_slot(jax.random.fold_in(seeds[8], 71), 0)
    prefix_len = draw_prefix_len(jax.random.fold_in(seeds[8], 71), 0)
    decode_page = draw_decode_page(jax.random.fold_in(seeds[8], 71), 0)
    out_weight = noise_with(seeds[7], (HEADS * HD, OUT_W), HEADS ** -0.5, 1.0, ((0, 8),), (0, 1, 8, 2.0))
    return dict(queries=queries, new_kv=new_kv, kv_pool=kv_pool, block_owner=block_owner, block_slot=block_slot, prefix_len=prefix_len, decode_page=decode_page, out_weight=out_weight)


def head_attention(query_rows, key_rows, value_rows, visible):
    scores = jnp.dot(query_rows, key_rows.T, preferred_element_type=jnp.float32) * (1.0 / math.sqrt(HD))
    scores = jnp.where(visible, scores, -jnp.inf)
    row_max = lax.optimization_barrier(jnp.max(scores, axis=1, keepdims=True))
    weights = jnp.exp(scores - row_max)
    row_total = lax.optimization_barrier(jnp.sum(weights, axis=1, keepdims=True))
    mixed_rows = jnp.dot(weights.astype(jnp.bfloat16), value_rows, preferred_element_type=jnp.float32)
    return (mixed_rows / row_total).astype(jnp.bfloat16)

def reference(queries, new_kv, kv_pool, block_owner, block_slot, prefix_len, decode_page, out_weight):
    page_index = (block_owner * POOL_DEV + block_slot).astype(jnp.int32)
    prefix_pos = jnp.arange(MAXBLK * PAGE, dtype=jnp.int32)
    new_pos = jnp.arange(NEW, dtype=jnp.int32)
    outputs = []
    for request in range(REQS):
        page_rows = jnp.take(kv_pool, page_index[request], axis=0)
        prefix_keys = jnp.transpose(page_rows[:, :, 0], (1, 0, 2, 3)).reshape(KV_HEADS, MAXBLK * PAGE, HD)
        prefix_values = jnp.transpose(page_rows[:, :, 1], (1, 0, 2, 3)).reshape(KV_HEADS, MAXBLK * PAGE, HD)
        key_all = jnp.concatenate([prefix_keys, new_kv[request, :, 0]], axis=1)
        value_all = jnp.concatenate([prefix_values, new_kv[request, :, 1]], axis=1)
        prefix_seen = jnp.broadcast_to((prefix_pos < prefix_len[request])[None, :], (NEW, MAXBLK * PAGE))
        visible = jnp.concatenate([prefix_seen, new_pos[None, :] <= new_pos[:, None]], axis=1)
        query_heads = jnp.transpose(queries[request].reshape(NEW, HEADS, HD), (1, 0, 2))

        def one_head(head_id):
            group_id = head_id // GROUP
            return head_attention(query_heads[head_id], key_all[group_id], value_all[group_id], visible)
        head_outs = lax.map(one_head, jnp.arange(HEADS, dtype=jnp.int32))
        outputs.append(jnp.transpose(head_outs, (1, 0, 2)).reshape(NEW, HEADS * HD))
    attention = jnp.stack(outputs).reshape(REQS * NEW, HEADS * HD)
    projected = jnp.dot(attention, out_weight, preferred_element_type=jnp.float32)
    attn_out = projected.astype(jnp.bfloat16).reshape(REQS, NEW, OUT_W)
    new_pages = jnp.transpose(new_kv.reshape(REQS, KV_HEADS, 2, NEWP, PAGE, HD), (0, 3, 1, 2, 4, 5))
    new_pages = new_pages.reshape(DEC_PAGES, KV_HEADS, 2, PAGE, HD)
    decode_cache = jnp.zeros_like(new_pages).at[decode_page.reshape(-1).astype(jnp.int32)].set(new_pages)
    return (attn_out, decode_cache)
```

```python
import functools

import jax
import jax.numpy as jnp
from jax import lax
from jax.experimental import pallas as pl
from jax.experimental.pallas import tpu as pltpu
from jax.sharding import PartitionSpec as P

MESH = pl.DeviceIdType.MESH
F32 = jnp.float32
BF16 = jnp.bfloat16
NY, NX, NH, NZ, NC = 4, 4, 2, 4, 2
PAGE = 128
HD = 128
GROUP = 8
ROWS = GROUP * PAGE
HALF = 512
KB = 1024
LIVE = 64
FULL = 48
SCALE = 1.4426950408889634 / HD**0.5
LOW = -1e30


def dot_t(a, b):
    return lax.dot_general(a, b, (((1,), (1,)), ((), ())), preferred_element_type=F32)


def dot_0(a, b):
    return lax.dot_general(a, b, (((0,), (0,)), ((), ())), preferred_element_type=F32)


def body(
    tab, q_ref, new_ref, pool_ref, w_hbm, out_ref, dec_ref,
    pages, news, qs, scores, acc, m_ref, l_ref, w_ref, att,
    sib_out, sib_in, chip, line_out, line_in, res,
    send, recv, z_send, z_recv, s_send, s_recv, t_send, t_recv, w_sem,
):
    p = lax.axis_index("pool")
    t = lax.axis_index("tp")
    y, x, h = p // (NX * NH), (p // NH) % NX, p % NH
    zl, core = t // NC, t % NC

    def at(yy, xx, hh):
        return {"pool": ((yy % NY) * NX + xx % NX) * NH + hh, "tp": t}

    w_copy = pltpu.make_async_copy(w_hbm, w_ref, w_sem)
    w_copy.start()

    barrier = pltpu.get_barrier_semaphore()
    partners = [at(y, x + d, h) for d in (1, 2, 3)]
    partners += [at(y + d, x, h) for d in (1, 2, 3)]
    partners += [at(y, x, 1 - h)]
    partners += [{"pool": p, "tp": zl * NC + 1 - core}]
    partners += [{"pool": p, "tp": ((zl + d) % NZ) * NC + core} for d in (1, 2, 3)]
    for device in partners:
        pl.semaphore_signal(barrier, inc=1, device_id=device, device_id_type=MESH)

    full = tab[LIVE + 3]
    for r in range(2):
        source = full if r == 0 else 1 - full
        for kv in range(2):
            news[r, kv, y, x, h] = new_ref[source, 0, kv]
        for g in range(GROUP):
            qs[r, g * PAGE:(g + 1) * PAGE, :] = q_ref[source, :, g * HD:(g + 1) * HD]
    for s in range(2):
        pages[s, y, x, h] = pool_ref[tab[LIVE + s], 0]
    pl.semaphore_wait(barrier, len(partners))

    def copy(ref, device, send_sem, recv_sem):
        return pltpu.make_async_remote_copy(
            src_ref=ref, dst_ref=ref, send_sem=send_sem, recv_sem=recv_sem,
            device_id=device, device_id_type=MESH,
        )

    def stage(phase, which):
        if phase < 2:
            hh = h if phase == 0 else 1 - h
            a_ref = pages.at[0, y, x, hh] if which == 0 else pages.at[0, y, :, hh]
            b_ref = pages.at[1, y, x, hh] if which == 0 else pages.at[1, :, x, hh]
        else:
            r = phase - 2
            a_ref = news.at[r, 0, y, x] if which == 0 else news.at[r, 0, y]
            b_ref = news.at[r, 1, y, x] if which == 0 else news.at[r, 1, :, x]
        copies = []
        for d in (1, 3, 2):
            i = (phase * 2 + which) * 6 + (d - 1) * 2
            by_x, by_y = at(y, x + d, h), at(y + d, x, h)
            first, second = (by_x, by_y) if which == 0 else (by_y, by_x)
            copies.append(copy(a_ref, first, send.at[i], recv.at[i]))
            copies.append(copy(b_ref, second, send.at[i + 1], recv.at[i + 1]))
        return copies

    def start(copies):
        for one in copies:
            one.start()

    def arrived(copies):
        for one in copies:
            one.wait_recv()

    across = [
        copy(pages.at[:, y, x, h], at(y, x, 1 - h), z_send.at[0], z_recv.at[0]),
        copy(news.at[:, :, y, x, h], at(y, x, 1 - h), z_send.at[1], z_recv.at[1]),
    ]
    stages = [[stage(phase, which) for which in range(2)] for phase in range(4)]
    start(stages[0][0])
    start(across)
    acc[...] = jnp.zeros_like(acc)
    m_ref[...] = jnp.full_like(m_ref, LOW)
    l_ref[...] = jnp.zeros_like(l_ref)
    arrived(stages[0][0])
    start(stages[0][1])
    arrived(across[:1])
    start(stages[1][0])
    arrived(stages[1][0])
    start(stages[1][1])
    arrived(across[1:])
    arrived(stages[0][1])
    start(stages[2][0])
    arrived(stages[2][0])
    start(stages[2][1])
    arrived(stages[1][1])
    start(stages[3][0])

    def produce(r, slot, keys):
        scores[slot] = dot_t(keys, qs[r, slot * HALF:(slot + 1) * HALF, :])

    def consume(r, slot, values, mask):
        cols = slice(slot * HALF, (slot + 1) * HALF)
        s = scores[slot]
        if mask is not None:
            s = jnp.where(mask, s, LOW)
        old = m_ref[r, :1, cols]
        top = jnp.maximum(old, jnp.max(s, axis=0, keepdims=True))
        weights = jnp.exp2((s - top) * SCALE)
        factor = jnp.exp2((old - top) * SCALE)
        l_ref[r, :1, cols] = l_ref[r, :1, cols] * factor + jnp.sum(weights, axis=0, keepdims=True)
        acc[r, :, cols] = acc[r, :, cols] * factor + dot_0(values, weights.astype(BF16))
        m_ref[r, :1, cols] = top

    def run(r, first, last, load, mask=None):
        produce(r, 0, load(first, 0))

        def step(i, carry):
            produce(r, 1, load(i, 0))
            consume(r, 0, load(i, 1), mask)
            produce(r, 0, load(jnp.minimum(i + 1, last - 1), 0))
            consume(r, 1, load(i, 1), mask)
            return carry

        lax.fori_loop(first, last, step, 0)

    def prefix(base):
        def load(i, kv):
            parts = []
            for j in range(KB // PAGE):
                where = tab[base + i * (KB // PAGE) + j]
                owner = where // 2
                parts.append(pages[where % 2, owner // (NX * NH), (owner // NH) % NX, owner % NH, kv])
            return jnp.concatenate(parts, axis=0)

        return load

    def new(r):
        def load(i, kv):
            return news[r, kv, i].reshape(KB, HD)

        return load

    run(0, 0, 3, prefix(0))
    arrived(stages[3][0])
    start(stages[3][1])
    run(0, 3, 6, prefix(0))
    run(1, 0, 1, prefix(FULL))
    key_pos = lax.broadcasted_iota(jnp.int32, (KB, HALF), 0)
    run(1, 1, 2, prefix(FULL), key_pos < tab[LIVE + 2] - KB)

    row_tok = lax.broadcasted_iota(jnp.int32, (KB, HALF), 1) % PAGE
    causal = key_pos <= row_tok + (p % (NX * NH)) * PAGE
    finals = []
    for r in range(2):
        arrived(stages[2 + r][1])

        @pl.when(y > 0)
        def _():
            run(r, 0, y, new(r))

        run(r, y, y + 1, new(r), causal)

        mixed = (acc[r] / l_ref[r, :1, :]).astype(BF16)
        for g in range(GROUP):
            att[:, g * HD:(g + 1) * HD] = mixed[:, g * PAGE:(g + 1) * PAGE].T
        if r == 0:
            w_copy.wait()

        def columns(which):
            def part(j, carry):
                at_col = pl.multiple_of((j * NC + which) * 512, 512)
                got = jnp.dot(att[...], w_ref[:, pl.ds(at_col, 512)], preferred_element_type=F32)
                return got

            return part

        def to_sib(j, carry):
            sib_out[r, j] = columns(1 - core)(j, 0).astype(BF16)
            return carry

        def to_own(j, carry):
            chip[j] = columns(core)(j, 0)
            return carry

        lax.fori_loop(0, NZ, to_sib, 0)
        sib = pltpu.make_async_remote_copy(
            src_ref=sib_out.at[r], dst_ref=sib_in.at[r], send_sem=s_send.at[r], recv_sem=s_recv.at[r],
            device_id={"pool": p, "tp": zl * NC + 1 - core}, device_id_type=MESH,
        )
        sib.start()
        lax.fori_loop(0, NZ, to_own, 0)
        sib.wait_recv()
        line = []
        for d in (2, 1, 3):
            other = (zl + d) % NZ
            line_out[r, d - 1] = (chip[other] + sib_in[r, other].astype(F32)).astype(BF16)
            i = r * 3 + d - 1
            one = pltpu.make_async_remote_copy(
                src_ref=line_out.at[r, d - 1], dst_ref=line_in.at[r, d - 1],
                send_sem=t_send.at[i], recv_sem=t_recv.at[i],
                device_id={"pool": p, "tp": other * NC + core}, device_id_type=MESH,
            )
            one.start()
            line.append(one)
        res[r] = chip[zl] + sib_in[r, zl].astype(F32)
        finals.append((sib, line))
        if r == 0:
            continue
        for s in range(2):
            where = tab[LIVE + 4 + s]
            owner = where % (NY * NX * NH)
            side = jnp.where(where // (NY * NX * NH) == full, 0, 1)
            for kv in range(2):
                dec_ref[s, 0, kv] = news[side, kv, owner // (NX * NH), (owner // NH) % NX, owner % NH]

    for r in range(2):
        sib, line = finals[r]
        arrived(line)
        total = res[r]
        for d in range(3):
            total = total + line_in[r, d].astype(F32)
        res[r] = total
    out_ref[0] = res[full].astype(BF16)
    out_ref[1] = res[1 - full].astype(BF16)

    for phase in range(4):
        for which in range(2):
            for one in stages[phase][which]:
                one.wait_send()
    for one in across:
        one.wait_send()
    for sib, line in finals:
        sib.wait_send()
        for one in line:
            one.wait_send()


def shards(queries, new_kv, kv_pool, block_owner, block_slot, prefix_len, decode_page, out_weight):
    me = lax.axis_index("pool")
    entries = jnp.arange(block_owner.shape[1], dtype=jnp.int32)[None, :]
    dead = (entries * PAGE >= prefix_len[:, None]).reshape(-1)
    owner = block_owner.reshape(-1)
    slot = block_slot.reshape(-1)
    same = (owner[:, None] == owner[None, :]) & dead[None, :]
    hole = jnp.sum(jnp.where(same, slot[None, :], 0), axis=1)
    where = (owner * 2 + slot - (slot > hole).astype(jnp.int32)).reshape(2, -1)
    full = jnp.where(prefix_len[0] == FULL * PAGE, 0, 1).astype(jnp.int32)
    mine = jnp.sum(jnp.where(dead & (owner == me), slot, 0))
    is_first = full == 0
    long_list = jnp.where(is_first, where[0], where[1])
    short_list = jnp.where(is_first, where[1], where[0])[: LIVE - FULL]
    short_len = jnp.where(is_first, prefix_len[1], prefix_len[0])
    flat_page = decode_page.reshape(-1)
    index = jnp.arange(flat_page.shape[0], dtype=jnp.int32)
    source = [jnp.sum(jnp.where(flat_page == me * 2 + s, index, 0)) for s in range(2)]
    scalars = jnp.stack([jnp.where(mine == 0, 1, 0), jnp.where(mine == 2, 1, 2), short_len, full, *source])
    table = jnp.concatenate([long_list, short_list, scalars]).astype(jnp.int32)

    vmem = pl.BlockSpec(memory_space=pltpu.VMEM)
    out, dec = pl.pallas_call(
        body,
        out_shape=(
            jax.ShapeDtypeStruct((2, PAGE, 512), BF16),
            jax.ShapeDtypeStruct((2, 1, 2, PAGE, HD), BF16),
        ),
        in_specs=[pl.BlockSpec(memory_space=pltpu.SMEM), vmem, vmem, vmem, pl.BlockSpec(memory_space=pl.ANY)],
        out_specs=(vmem, vmem),
        scratch_shapes=[
            pltpu.VMEM((2, NY, NX, NH, 2, PAGE, HD), BF16),
            pltpu.VMEM((2, 2, NY, NX, NH, PAGE, HD), BF16),
            pltpu.VMEM((2, ROWS, HD), BF16),
            pltpu.VMEM((2, KB, HALF), F32),
            pltpu.VMEM((2, HD, ROWS), F32),
            pltpu.VMEM((2, 8, ROWS), F32),
            pltpu.VMEM((2, 8, ROWS), F32),
            pltpu.VMEM((GROUP * HD, 4096), BF16),
            pltpu.VMEM((PAGE, GROUP * HD), BF16),
            pltpu.VMEM((2, NZ, PAGE, 512), BF16),
            pltpu.VMEM((2, NZ, PAGE, 512), BF16),
            pltpu.VMEM((NZ, PAGE, 512), F32),
            pltpu.VMEM((2, 3, PAGE, 512), BF16),
            pltpu.VMEM((2, 3, PAGE, 512), BF16),
            pltpu.VMEM((2, PAGE, 512), F32),
            pltpu.SemaphoreType.DMA((48,)),
            pltpu.SemaphoreType.DMA((48,)),
            pltpu.SemaphoreType.DMA((2,)),
            pltpu.SemaphoreType.DMA((2,)),
            pltpu.SemaphoreType.DMA((2,)),
            pltpu.SemaphoreType.DMA((2,)),
            pltpu.SemaphoreType.DMA((6,)),
            pltpu.SemaphoreType.DMA((6,)),
            pltpu.SemaphoreType.DMA,
        ],
        compiler_params=pltpu.CompilerParams(
            collective_id=0, has_side_effects=True, vmem_limit_bytes=56 << 20
        ),
        cost_estimate=pl.CostEstimate(flops=11 * 10**9, bytes_accessed=10 << 20, transcendentals=16 << 20),
        name="paged_prefill",
    )(table, queries, new_kv, kv_pool, out_weight)
    return out, dec


def solution(mesh):
    return jax.shard_map(
        shards,
        mesh=mesh,
        in_specs=(
            P(None, "pool", "tp"),
            P(None, "tp", None, "pool", None),
            P("pool", "tp", None, None, None),
            P(),
            P(),
            P(),
            P(),
            P("tp", None),
        ),
        out_specs=(P(None, "pool", "tp"), P("pool", "tp", None, None, None)),
        check_vma=False,
    )
```

```python
import functools

import jax
import jax.numpy as jnp
from jax import lax
from jax.experimental import pallas as pl
from jax.experimental.pallas import tpu as pltpu
from jax.sharding import PartitionSpec as P

MESH = pl.DeviceIdType.MESH
F32 = jnp.float32
BF16 = jnp.bfloat16
NY, NX, NH, NZ, NC = 4, 4, 2, 4, 2
PAGE = 128
HD = 128
GROUP = 8
ROWS = GROUP * PAGE
HALF = 512
KB = 1024
LIVE = 64
FULL = 48
SCALE = 1.4426950408889634 / HD**0.5
LOW = -1e30


def dot_t(a, b):
    return lax.dot_general(a, b, (((1,), (1,)), ((), ())), preferred_element_type=F32)


def dot_0(a, b):
    return lax.dot_general(a, b, (((0,), (0,)), ((), ())), preferred_element_type=F32)


def body(
    len_ref, own_ref, slot_ref, dpage_ref, q_hbm, new_ref, pool_ref, w_hbm, out_ref, dec_ref,
    near, far, news, q_v, qs, scores, acc, m_ref, l_ref, w_ref, att,
    sib_out, sib_in, line_out, line_in, res, tab_v, tab,
    send, recv, z_send, z_recv, s_send, s_recv, t_send, t_recv, w_sem, tab_sem, q_sem,
):
    p = lax.axis_index("pool")
    t = lax.axis_index("tp")
    y, x, h = p // (NX * NH), (p // NH) % NX, p % NH
    zl, core = t // NC, t % NC

    def at(yy, xx, hh):
        return {"pool": (((yy + NY) % NY) * NX + (xx + NX) % NX) * NH + hh, "tp": t}

    w_copy = pltpu.make_async_copy(w_hbm, w_ref, w_sem)
    w_copy.start()
    q_copy = pltpu.make_async_copy(q_hbm, q_v, q_sem)
    q_copy.start()

    barrier = pltpu.get_barrier_semaphore()
    partners = [at(y, x + d, h) for d in (1, 2, 3)]
    partners += [at(y + d, x, h) for d in (1, 2, 3)]
    partners += [at(y, x, 1 - h)]
    partners += [{"pool": p, "tp": zl * NC + 1 - core}]
    beside, opposite = zl + 1 - 2 * (zl % 2), (zl + 2) % NZ
    partners += [{"pool": p, "tp": z * NC + core} for z in (beside, opposite)]
    for device in partners:
        pl.semaphore_signal(barrier, inc=1, device_id=device, device_id_type=MESH)

    full = jnp.where(len_ref[0] == FULL * PAGE, 0, 1)
    short_len = len_ref[1 - full]

    entry = lax.broadcasted_iota(jnp.int32, (1, FULL), 1)
    device_row = lax.broadcasted_iota(jnp.int32, (NY * NX * NH, FULL), 0)
    owners = [own_ref[r:r + 1, :] for r in range(2)]
    slots = [slot_ref[r:r + 1, :] for r in range(2)]
    dead = [entry * PAGE >= len_ref[r] for r in range(2)]
    holes = jnp.zeros((NY * NX * NH, 1), jnp.int32)
    mine = jnp.int32(0)
    for r in range(2):
        dead_slot = jnp.where(dead[r], slots[r], 0)
        holes = holes + jnp.sum(jnp.where(owners[r] == device_row, dead_slot, 0), axis=1, keepdims=True)
        mine = mine + jnp.sum(jnp.where(owners[r] == p, dead_slot, 0))
    first_slot = jnp.where(mine == 0, 1, 0)
    second_slot = jnp.where(mine == 2, 1, 2)
    for s, chosen in enumerate((first_slot, second_slot)):
        near[s, y, x] = pool_ref[chosen, 0]

    def copy(ref, device, send_sem, recv_sem, there=None):
        return pltpu.make_async_remote_copy(
            src_ref=ref, dst_ref=ref if there is None else there, send_sem=send_sem, recv_sem=recv_sem,
            device_id=device, device_id_type=MESH,
        )

    def start(copies):
        for one in copies:
            one.start()

    def arrived(copies):
        for one in copies:
            one.wait_recv()

    def phase_copies(phase):
        if phase < 2:
            held = near if phase == 0 else far

            def a_item(yy, xx, part=None):
                ref = held.at[0, yy, xx]
                return ref if part is None else ref.at[part]

            def b_item(yy, xx, part=None):
                ref = held.at[1, yy, xx]
                return ref if part is None else ref.at[part]
        else:

            def a_item(yy, xx, part=None):
                ref = news.at[phase - 2, 0, yy, xx]
                return ref if part is None else ref.at[part]

            def b_item(yy, xx, part=None):
                ref = news.at[phase - 2, 1, yy, xx]
                return ref if part is None else ref.at[part]

        count = [phase * 40]

        def one(ref, device):
            i = count[0]
            count[0] += 1
            return copy(ref, device, send.at[i], recv.at[i])

        def wrap(v, n):
            return (v + n) % n

        steps = {}
        steps["s1"] = []
        for d in (1, 3, 2):
            steps["s1"] += [one(a_item(y, x), at(y, x + d, h)), one(b_item(y, x), at(y + d, x, h))]
        for k in range(4):
            xx, yy = wrap(x + k, NX), wrap(y + k, NY)
            steps["g%d" % k] = [
                one(a_item(y, xx), at(y + 1, x, h)), one(a_item(y, xx), at(y - 1, x, h)),
                one(b_item(yy, x), at(y, x + 1, h)), one(b_item(yy, x), at(y, x - 1, h)),
            ]
            steps["f2%d" % k] = [
                one(a_item(wrap(y - 1, NY), xx, 0), at(y + 1, x, h)),
                one(a_item(wrap(y + 1, NY), xx, 1), at(y - 1, x, h)),
                one(b_item(yy, wrap(x - 1, NX), 0), at(y, x + 1, h)),
                one(b_item(yy, wrap(x + 1, NX), 1), at(y, x - 1, h)),
            ]
        return steps

    phases = [phase_copies(phase) for phase in range(4)]
    across = [
        copy(near.at[:, y, x], at(y, x, 1 - h), z_send.at[0], z_recv.at[0], far.at[:, y, x]),
        copy(news.at[0, :, y, x, h], at(y, x, 1 - h), z_send.at[1], z_recv.at[1]),
        copy(news.at[1, :, y, x, h], at(y, x, 1 - h), z_send.at[2], z_recv.at[2]),
    ]

    def begin(n):
        if n > 0:
            arrived(across[n - 1:n])
        start(phases[n]["s1"])
        start(phases[n]["g0"])

    def event(n, what):
        ph = phases[n]
        if what == 0:
            arrived(ph["s1"])
            for k in (1, 3, 2):
                start(ph["g%d" % k])
        elif what < 5:
            k = (0, 1, 3, 2)[what - 1]
            arrived(ph["g%d" % k])
            start(ph["f2%d" % k])
        else:
            for k in range(4):
                arrived(ph["f2%d" % k])

    pl.semaphore_wait(barrier, len(partners))
    start(phases[0]["s1"])
    start(across[:1])
    start(phases[0]["g0"])
    for r in range(2):
        for kv in range(2):
            news[r, kv, y, x, h] = new_ref[full if r == 0 else 1 - full, 0, kv]
    start(across[1:])
    q_copy.wait()
    for r in range(2):
        source = full if r == 0 else 1 - full
        for g in range(GROUP):
            qs[r, g * PAGE:(g + 1) * PAGE, :] = q_v[source, :, g * HD:(g + 1) * HD]

    def turned(row):
        n = row.shape[1]
        rows = lax.broadcasted_iota(jnp.int32, (n, n), 0)
        lanes = lax.broadcasted_iota(jnp.int32, (n, n), 1)
        return jnp.sum(jnp.where(rows == lanes, row, 0), axis=1, keepdims=True)

    spots = []
    for r in range(2):
        hole = jnp.sum(jnp.where(owners[r] == device_row, holes, 0), axis=0, keepdims=True)
        spots.append((slots[r] - (slots[r] > hole).astype(jnp.int32)) * (NY * NX * NH) + owners[r])
    first_full = full == 0
    long_spots = jnp.where(first_full, spots[0], spots[1])
    short_spots = jnp.where(first_full, spots[1], spots[0])
    long_near = (long_spots % NH == h).astype(jnp.int32)
    near_col = turned(long_near)
    spot_col = turned(long_spots)
    rows = lax.broadcasted_iota(jnp.int32, (FULL, FULL), 0)
    lanes = lax.broadcasted_iota(jnp.int32, (FULL, FULL), 1)
    before_near = jnp.sum(jnp.where(lanes < rows, long_near, 0), axis=1, keepdims=True)
    all_near = jnp.sum(long_near, axis=1, keepdims=True)
    rank = jnp.where(near_col == 1, before_near, all_near + rows[:, :1] - before_near)
    ordered = jnp.sum(jnp.where(rank == lanes, spot_col, 0), axis=0, keepdims=True)
    tab_v[0:1, 0:FULL] = ordered
    tab_v[1:2, 0:FULL] = short_spots
    tab_copy = pltpu.make_async_copy(tab_v, tab, tab_sem)
    tab_copy.start()
    acc[...] = jnp.zeros_like(acc)
    m_ref[...] = jnp.full_like(m_ref, LOW)
    l_ref[...] = jnp.zeros_like(l_ref)

    def produce(r, slot, keys):
        scores[slot] = dot_t(keys, qs[r, slot * HALF:(slot + 1) * HALF, :])

    def consume(r, slot, values, mask):
        cols = slice(slot * HALF, (slot + 1) * HALF)
        s = scores[slot]
        if mask is not None:
            s = jnp.where(mask, s, LOW)
        old = m_ref[r, :1, cols]
        top = jnp.maximum(old, jnp.max(s, axis=0, keepdims=True))
        weights = jnp.exp2((s - top) * SCALE)
        factor = jnp.exp2((old - top) * SCALE)
        l_ref[r, :1, cols] = l_ref[r, :1, cols] * factor + jnp.sum(weights, axis=0, keepdims=True)
        acc[r, :, cols] = acc[r, :, cols] * factor + dot_0(values, weights.astype(BF16))
        m_ref[r, :1, cols] = top

    def run(blocks, services=()):
        services = list(services)
        halves = [(block, slot) for block in blocks for slot in range(2)]
        produce(halves[0][0][0], 0, halves[0][0][1](0))
        for n, ((r, load, mask), slot) in enumerate(halves):
            if n + 1 < len(halves):
                (r2, load2, mask2), slot2 = halves[n + 1]
                produce(r2, slot2, load2(0))
            consume(r, slot, load(1), mask)
            if services:
                for one in services.pop(0):
                    event(*one)
        assert not services

    def prefix(which, i, near_only=False):
        def load(kv):
            parts = []
            for j in range(KB // PAGE):
                where = tab[which, i * (KB // PAGE) + j]
                spot = (where // (NY * NX * NH), (where // (NX * NH)) % NY, (where // NH) % NX, kv)
                part = near[spot]
                if not near_only:
                    part = jnp.where(where % NH == h, part, far[spot])
                parts.append(part)
            return jnp.concatenate(parts, axis=0)

        return load

    def new(r, row):
        def load(kv):
            return news[r, kv, row].reshape(KB, HD)

        return load

    event(0, 0)
    begin(1)
    event(0, 1)
    event(0, 2)
    event(0, 3)
    event(1, 0)
    event(0, 4)
    tab_copy.wait()
    event(0, 5)
    begin(2)
    run([(0, prefix(0, i, True), None) for i in range(2)], [[(1, 1)], [(1, 2)], [(1, 3)], [(1, 4)]])
    event(2, 0)
    event(1, 5)
    begin(3)
    key_pos = lax.broadcasted_iota(jnp.int32, (KB, HALF), 0)
    row_tok = lax.broadcasted_iota(jnp.int32, (KB, HALF), 1) % PAGE
    in_short = key_pos < short_len - KB
    causal = key_pos <= row_tok + (p % (NX * NH)) * PAGE
    run(
        [(0, prefix(0, i), None) for i in range(2, 6)] + [(1, prefix(1, 0), None), (1, prefix(1, 1), in_short)],
        [[], [(2, 1)], [], [(2, 2)], [], [(2, 3)], [], [(2, 4)], [], [(3, 0)], [], [(3, 1)]],
    )

    finals = []
    for r in range(2):
        event(2 + r, 5)
        run([(r, new(r, y), causal)], [[], [(3, 2)]] if r == 0 else [])
        if r == 1:
            finals[0][2]()
        for k in (1, 2, 3):

            @pl.when(y >= k)
            def _():
                run([(r, new(r, y - k), None)])

            if r == 0 and k < 3:
                event(3, 2 + k)

        mixed = (acc[r] / l_ref[r, :1, :]).astype(BF16)
        for g in range(GROUP):
            att[:, g * HD:(g + 1) * HD] = mixed[:, g * PAGE:(g + 1) * PAGE].T
        if r == 0:
            w_copy.wait()

        def block(j, which):
            at_col = pl.multiple_of((j * NC + which) * 512, 512)
            return jnp.dot(att[...], w_ref[:, pl.ds(at_col, 512)], preferred_element_type=F32)

        dests = [NZ - 1 - zl, beside, opposite, zl]
        sibs, line = [], []

        def give(n):
            i = r * NZ + n
            sib_out[i] = block(dests[n], 1 - core).astype(BF16)
            one = pltpu.make_async_remote_copy(
                src_ref=sib_out.at[i], dst_ref=sib_in.at[i], send_sem=s_send.at[i], recv_sem=s_recv.at[i],
                device_id={"pool": p, "tp": zl * NC + 1 - core}, device_id_type=MESH,
            )
            one.start()
            sibs.append(one)

        def send_line(n, device, r=r, line=line):
            i = r * NZ + n
            one = pltpu.make_async_remote_copy(
                src_ref=line_out.at[i], dst_ref=line_in.at[i], send_sem=t_send.at[i], recv_sem=t_recv.at[i],
                device_id={"pool": p, "tp": device * NC + core}, device_id_type=MESH,
            )
            one.start()
            line.append(one)

        def pass_on(n):
            total = block(dests[n], core)
            sibs[n].wait_recv()
            total = total + sib_in[r * NZ + n].astype(F32)
            if n < 2:
                line_out[r * NZ + n] = total.astype(BF16)
                send_line(n, beside)
            else:
                res[r, n - 2] = total

        def relay(r=r, line=line, send_line=send_line):
            line[0].wait_recv()
            line_out[r * NZ + 2] = (res[r, 0] + line_in[r * NZ].astype(F32)).astype(BF16)
            send_line(2, opposite)

        give(0)
        give(1)
        pass_on(0)
        give(2)
        pass_on(1)
        give(3)
        pass_on(2)
        if r == 1:
            relay()
        pass_on(3)
        finals.append((sibs, line, relay))
        if r == 0:
            continue
        page_at = lax.broadcasted_iota(jnp.int32, dpage_ref.shape, 1)
        page_of = lax.broadcasted_iota(jnp.int32, dpage_ref.shape, 0)
        for s in range(2):
            chosen = dpage_ref[...] == p * 2 + s
            owner = jnp.minimum(jnp.sum(jnp.where(chosen, page_at, 0)), NY * NX * NH - 1)
            side = jnp.where(jnp.sum(jnp.where(chosen, page_of, 0)) == full, 0, 1)
            for kv in range(2):
                dec_ref[s, 0, kv] = news[side, kv, owner // (NX * NH), (owner // NH) % NX, owner % NH]

    for r in range(2):
        sibs, line, _ = finals[r]
        arrived(line[1:])
        res[r, 1] = res[r, 1] + line_in[r * NZ + 1].astype(F32) + line_in[r * NZ + 2].astype(F32)
    out_ref[0] = res[full, 1].astype(BF16)
    out_ref[1] = res[1 - full, 1].astype(BF16)

    for ph in phases:
        for copies in ph.values():
            for one in copies:
                one.wait_send()
    for one in across:
        one.wait_send()
    for sibs, line, _ in finals:
        for one in sibs + line:
            one.wait_send()


def shards(queries, new_kv, kv_pool, block_owner, block_slot, prefix_len, decode_page, out_weight):
    vmem = pl.BlockSpec(memory_space=pltpu.VMEM)
    any_space = pl.BlockSpec(memory_space=pl.ANY)
    out, dec = pl.pallas_call(
        body,
        out_shape=(
            jax.ShapeDtypeStruct((2, PAGE, 512), BF16),
            jax.ShapeDtypeStruct((2, 1, 2, PAGE, HD), BF16),
        ),
        in_specs=[pl.BlockSpec(memory_space=pltpu.SMEM)] + [vmem] * 3 + [any_space] + [vmem] * 2 + [any_space],
        out_specs=(vmem, vmem),
        scratch_shapes=[
            pltpu.VMEM((2, NY, NX, 2, PAGE, HD), BF16),
            pltpu.VMEM((2, NY, NX, 2, PAGE, HD), BF16),
            pltpu.VMEM((2, 2, NY, NX, NH, PAGE, HD), BF16),
            pltpu.VMEM((2, PAGE, GROUP * HD), BF16),
            pltpu.VMEM((2, ROWS, HD), BF16),
            pltpu.VMEM((2, KB, HALF), F32),
            pltpu.VMEM((2, HD, ROWS), F32),
            pltpu.VMEM((2, 8, ROWS), F32),
            pltpu.VMEM((2, 8, ROWS), F32),
            pltpu.VMEM((GROUP * HD, 4096), BF16),
            pltpu.VMEM((PAGE, GROUP * HD), BF16),
            pltpu.VMEM((2 * NZ, PAGE, 512), BF16),
            pltpu.VMEM((2 * NZ, PAGE, 512), BF16),
            pltpu.VMEM((2 * NZ, PAGE, 512), BF16),
            pltpu.VMEM((2 * NZ, PAGE, 512), BF16),
            pltpu.VMEM((2, 2, PAGE, 512), F32),
            pltpu.VMEM((8, 128), jnp.int32),
            pltpu.SMEM((8, 128), jnp.int32),
            pltpu.SemaphoreType.DMA((160,)),
            pltpu.SemaphoreType.DMA((160,)),
            pltpu.SemaphoreType.DMA((3,)),
            pltpu.SemaphoreType.DMA((3,)),
            pltpu.SemaphoreType.DMA((8,)),
            pltpu.SemaphoreType.DMA((8,)),
            pltpu.SemaphoreType.DMA((8,)),
            pltpu.SemaphoreType.DMA((8,)),
            pltpu.SemaphoreType.DMA,
            pltpu.SemaphoreType.DMA,
            pltpu.SemaphoreType.DMA,
        ],
        compiler_params=pltpu.CompilerParams(
            collective_id=0, has_side_effects=True, vmem_limit_bytes=56 << 20
        ),
        cost_estimate=pl.CostEstimate(flops=11 * 10**9, bytes_accessed=10 << 20, transcendentals=16 << 20),
        name="paged_prefill",
    )(prefix_len, block_owner, block_slot, decode_page, queries, new_kv, kv_pool, out_weight)
    return out, dec


def solution(mesh):
    return jax.shard_map(
        shards,
        mesh=mesh,
        in_specs=(
            P(None, "pool", "tp"),
            P(None, "tp", None, "pool", None),
            P("pool", "tp", None, None, None),
            P(),
            P(),
            P(),
            P(),
            P("tp", None),
        ),
        out_specs=(P(None, "pool", "tp"), P("pool", "tp", None, None, None)),
        check_vma=False,
    )
```

```python
import functools

import jax
import jax.numpy as jnp
from jax import lax
from jax.experimental import pallas as pl
from jax.experimental.pallas import tpu as pltpu
from jax.sharding import PartitionSpec as P

MESH = pl.DeviceIdType.MESH
F32 = jnp.float32
BF16 = jnp.bfloat16
NY, NX, NH, NZ, NC = 4, 4, 2, 4, 2
PAGE = 128
HD = 128
GROUP = 8
ROWS = GROUP * PAGE
HALF = 512
KB = 1024
LIVE = 64
FULL = 48
SCALE = 1.4426950408889634 / HD**0.5
LOW = -1e30


def dot_t(a, b):
    return lax.dot_general(a, b, (((1,), (1,)), ((), ())), preferred_element_type=F32)


def dot_0(a, b):
    return lax.dot_general(a, b, (((0,), (0,)), ((), ())), preferred_element_type=F32)


def body(
    len_ref, own_ref, slot_ref, dpage_ref, q_hbm, new_ref, pool_ref, w_hbm, out_ref, dec_ref,
    near, far, news, q_v, qs, scores, acc, m_ref, l_ref, w_ref, att,
    sib_out, sib_in, line_out, line_in, res, tab_v, tab,
    send, recv, z_send, z_recv, s_send, s_recv, t_send, t_recv, w_sem, tab_sem, q_sem,
):
    p = lax.axis_index("pool")
    t = lax.axis_index("tp")
    y, x, h = p // (NX * NH), (p // NH) % NX, p % NH
    zl, core = t // NC, t % NC

    def at(yy, xx, hh):
        return {"pool": (((yy + NY) % NY) * NX + (xx + NX) % NX) * NH + hh, "tp": t}

    w_copy = pltpu.make_async_copy(w_hbm, w_ref, w_sem)
    w_copy.start()
    q_copy = pltpu.make_async_copy(q_hbm, q_v, q_sem)
    q_copy.start()

    barrier = pltpu.get_barrier_semaphore()
    partners = [at(y, x + d, h) for d in (1, 2, 3)]
    partners += [at(y + d, x, h) for d in (1, 2, 3)]
    partners += [at(y, x, 1 - h)]
    partners += [{"pool": p, "tp": zl * NC + 1 - core}]
    beside, opposite = zl + 1 - 2 * (zl % 2), (zl + 2) % NZ
    partners += [{"pool": p, "tp": z * NC + core} for z in (beside, opposite)]
    for device in partners:
        pl.semaphore_signal(barrier, inc=1, device_id=device, device_id_type=MESH)

    full = jnp.where(len_ref[0] == FULL * PAGE, 0, 1)
    short_len = len_ref[1 - full]

    entry = lax.broadcasted_iota(jnp.int32, (1, FULL), 1)
    device_row = lax.broadcasted_iota(jnp.int32, (NY * NX * NH, FULL), 0)
    owners = [own_ref[r:r + 1, :] for r in range(2)]
    slots = [slot_ref[r:r + 1, :] for r in range(2)]
    dead = [entry * PAGE >= len_ref[r] for r in range(2)]
    holes = jnp.zeros((NY * NX * NH, 1), jnp.int32)
    mine = jnp.int32(0)
    for r in range(2):
        dead_slot = jnp.where(dead[r], slots[r], 0)
        holes = holes + jnp.sum(jnp.where(owners[r] == device_row, dead_slot, 0), axis=1, keepdims=True)
        mine = mine + jnp.sum(jnp.where(owners[r] == p, dead_slot, 0))
    first_slot = jnp.where(mine == 0, 1, 0)
    second_slot = jnp.where(mine == 2, 1, 2)
    for s, chosen in enumerate((first_slot, second_slot)):
        near[s, y, x] = pool_ref[chosen, 0]

    def copy(ref, device, send_sem, recv_sem, there=None):
        return pltpu.make_async_remote_copy(
            src_ref=ref, dst_ref=ref if there is None else there, send_sem=send_sem, recv_sem=recv_sem,
            device_id=device, device_id_type=MESH,
        )

    def start(copies):
        for one in copies:
            one.start()

    def arrived(copies):
        for one in copies:
            one.wait_recv()

    def phase_copies(phase):
        if phase < 2:
            held = near if phase == 0 else far

            def a_item(yy, xx, part=None):
                ref = held.at[0, yy, xx]
                return ref if part is None else ref.at[part]

            def b_item(yy, xx, part=None):
                ref = held.at[1, yy, xx]
                return ref if part is None else ref.at[part]
        else:

            def a_item(yy, xx, part=None):
                ref = news.at[phase - 2, 0, yy, xx]
                return ref if part is None else ref.at[part]

            def b_item(yy, xx, part=None):
                ref = news.at[phase - 2, 1, yy, xx]
                return ref if part is None else ref.at[part]

        count = [phase * 40]

        def one(ref, device):
            i = count[0]
            count[0] += 1
            return copy(ref, device, send.at[i], recv.at[i])

        def wrap(v, n):
            return (v + n) % n

        steps = {}
        steps["s1"] = []
        for d in (1, 3, 2):
            steps["s1"] += [one(a_item(y, x), at(y, x + d, h)), one(b_item(y, x), at(y + d, x, h))]
        for k in range(4):
            xx, yy = wrap(x + k, NX), wrap(y + k, NY)
            steps["g%d" % k] = [
                one(a_item(y, xx), at(y + 1, x, h)), one(a_item(y, xx), at(y - 1, x, h)),
                one(b_item(yy, x), at(y, x + 1, h)), one(b_item(yy, x), at(y, x - 1, h)),
            ]
            steps["f2%d" % k] = [
                one(a_item(wrap(y - 1, NY), xx, 0), at(y + 1, x, h)),
                one(a_item(wrap(y + 1, NY), xx, 1), at(y - 1, x, h)),
                one(b_item(yy, wrap(x - 1, NX), 0), at(y, x + 1, h)),
                one(b_item(yy, wrap(x + 1, NX), 1), at(y, x - 1, h)),
            ]
        return steps

    phases = [phase_copies(phase) for phase in range(4)]
    across = [
        copy(near.at[:, y, x], at(y, x, 1 - h), z_send.at[0], z_recv.at[0], far.at[:, y, x]),
        copy(news.at[0, :, y, x, h], at(y, x, 1 - h), z_send.at[1], z_recv.at[1]),
        copy(news.at[1, :, y, x, h], at(y, x, 1 - h), z_send.at[2], z_recv.at[2]),
    ]

    def begin(n):
        if n > 0:
            arrived(across[n - 1:n])
        start(phases[n]["s1"])
        start(phases[n]["g0"])

    def event(n, what):
        ph = phases[n]
        if what == 0:
            arrived(ph["s1"])
            for k in (1, 3, 2):
                start(ph["g%d" % k])
        elif what < 5:
            k = (0, 1, 3, 2)[what - 1]
            arrived(ph["g%d" % k])
            start(ph["f2%d" % k])
        else:
            for k in range(4):
                arrived(ph["f2%d" % k])

    pl.semaphore_wait(barrier, len(partners))
    start(phases[0]["s1"])
    start(across[:1])
    start(phases[0]["g0"])
    for r in range(2):
        for kv in range(2):
            news[r, kv, y, x, h] = new_ref[full if r == 0 else 1 - full, 0, kv]
    start(across[1:])
    q_copy.wait()
    for r in range(2):
        source = full if r == 0 else 1 - full
        for g in range(GROUP):
            qs[r, g * PAGE:(g + 1) * PAGE, :] = q_v[source, :, g * HD:(g + 1) * HD]

    def turned(row):
        n = row.shape[1]
        rows = lax.broadcasted_iota(jnp.int32, (n, n), 0)
        lanes = lax.broadcasted_iota(jnp.int32, (n, n), 1)
        return jnp.sum(jnp.where(rows == lanes, row, 0), axis=1, keepdims=True)

    spots = []
    for r in range(2):
        hole = jnp.sum(jnp.where(owners[r] == device_row, holes, 0), axis=0, keepdims=True)
        spots.append((slots[r] - (slots[r] > hole).astype(jnp.int32)) * (NY * NX * NH) + owners[r])
    first_full = full == 0
    long_spots = jnp.where(first_full, spots[0], spots[1])
    short_spots = jnp.where(first_full, spots[1], spots[0])
    long_near = (long_spots % NH == h).astype(jnp.int32)
    near_col = turned(long_near)
    spot_col = turned(long_spots)
    rows = lax.broadcasted_iota(jnp.int32, (FULL, FULL), 0)
    lanes = lax.broadcasted_iota(jnp.int32, (FULL, FULL), 1)
    before_near = jnp.sum(jnp.where(lanes < rows, long_near, 0), axis=1, keepdims=True)
    all_near = jnp.sum(long_near, axis=1, keepdims=True)
    rank = jnp.where(near_col == 1, before_near, all_near + rows[:, :1] - before_near)
    ordered = jnp.sum(jnp.where(rank == lanes, spot_col, 0), axis=0, keepdims=True)
    tab_v[0:1, 0:FULL] = ordered
    tab_v[1:2, 0:FULL] = short_spots
    tab_copy = pltpu.make_async_copy(tab_v, tab, tab_sem)
    tab_copy.start()
    acc[...] = jnp.zeros_like(acc)
    m_ref[...] = jnp.full_like(m_ref, LOW)
    l_ref[...] = jnp.zeros_like(l_ref)

    def produce(r, slot, keys):
        scores[slot] = dot_t(keys, qs[r, slot * HALF:(slot + 1) * HALF, :])

    def consume(r, slot, values, mask):
        cols = slice(slot * HALF, (slot + 1) * HALF)
        s = scores[slot]
        if mask is not None:
            s = jnp.where(mask, s, LOW)
        old = m_ref[r, :1, cols]
        top = jnp.maximum(old, jnp.max(s, axis=0, keepdims=True))
        weights = jnp.exp2((s - top) * SCALE)
        factor = jnp.exp2((old - top) * SCALE)
        l_ref[r, :1, cols] = l_ref[r, :1, cols] * factor + jnp.sum(weights, axis=0, keepdims=True)
        acc[r, :, cols] = acc[r, :, cols] * factor + dot_0(values, weights.astype(BF16))
        m_ref[r, :1, cols] = top

    def run(blocks, services=()):
        services = list(services)
        halves = [(block, slot) for block in blocks for slot in range(2)]
        produce(halves[0][0][0], 0, halves[0][0][1](0))
        for n, ((r, load, mask), slot) in enumerate(halves):
            if n + 1 < len(halves):
                (r2, load2, mask2), slot2 = halves[n + 1]
                produce(r2, slot2, load2(0))
            consume(r, slot, load(1), mask)
            if services:
                for one in services.pop(0):
                    event(*one)
        assert not services

    def prefix(which, i, near_only=False):
        def load(kv):
            parts = []
            for j in range(KB // PAGE):
                where = tab[which, i * (KB // PAGE) + j]
                spot = (where // (NY * NX * NH), (where // (NX * NH)) % NY, (where // NH) % NX, kv)
                part = near[spot]
                if not near_only:
                    part = jnp.where(where % NH == h, part, far[spot])
                parts.append(part)
            return jnp.concatenate(parts, axis=0)

        return load

    def new(r, row):
        def load(kv):
            return news[r, kv, row].reshape(KB, HD)

        return load

    event(0, 0)
    begin(1)
    event(0, 1)
    event(0, 2)
    event(0, 3)
    event(1, 0)
    event(0, 4)
    tab_copy.wait()
    event(0, 5)
    begin(2)
    run([(0, prefix(0, i, True), None) for i in range(2)], [[(1, 1)], [(1, 2)], [(1, 3)], [(1, 4)]])
    event(2, 0)
    event(1, 5)
    begin(3)
    key_pos = lax.broadcasted_iota(jnp.int32, (KB, HALF), 0)
    row_tok = lax.broadcasted_iota(jnp.int32, (KB, HALF), 1) % PAGE
    in_short = key_pos < short_len - KB
    causal = key_pos <= row_tok + (p % (NX * NH)) * PAGE
    run(
        [(0, prefix(0, i), None) for i in range(2, 6)] + [(1, prefix(1, 0), None), (1, prefix(1, 1), in_short)],
        [[], [(2, 1)], [], [(2, 2)], [], [(2, 3)], [], [(2, 4)], [], [(3, 0)], [], [(3, 1)]],
    )

    finals = []
    for r in range(2):
        event(2 + r, 5)
        run([(r, new(r, y), causal)], [[], [(3, 2)]] if r == 0 else [])
        if r == 1:
            finals[0][2]()
        for k in (1, 2, 3):

            @pl.when(y >= k)
            def _():
                run([(r, new(r, y - k), None)])

            if r == 0 and k < 3:
                event(3, 2 + k)

        mixed = (acc[r] / l_ref[r, :1, :]).astype(BF16)
        for g in range(GROUP):
            att[:, g * HD:(g + 1) * HD] = mixed[:, g * PAGE:(g + 1) * PAGE].T
        if r == 0:
            w_copy.wait()

        def block(j, which):
            at_col = pl.multiple_of((j * NC + which) * 512, 512)
            return jnp.dot(att[...], w_ref[:, pl.ds(at_col, 512)], preferred_element_type=F32)

        dests = [NZ - 1 - zl, beside, opposite, zl]
        sibs, line = [], []

        def give(n):
            i = r * NZ + n
            sib_out[i] = block(dests[n], 1 - core).astype(BF16)
            one = pltpu.make_async_remote_copy(
                src_ref=sib_out.at[i], dst_ref=sib_in.at[i], send_sem=s_send.at[i], recv_sem=s_recv.at[i],
                device_id={"pool": p, "tp": zl * NC + 1 - core}, device_id_type=MESH,
            )
            one.start()
            sibs.append(one)

        def send_line(n, device, r=r, line=line):
            i = r * NZ + n
            one = pltpu.make_async_remote_copy(
                src_ref=line_out.at[i], dst_ref=line_in.at[i], send_sem=t_send.at[i], recv_sem=t_recv.at[i],
                device_id={"pool": p, "tp": device * NC + core}, device_id_type=MESH,
            )
            one.start()
            line.append(one)

        def pass_on(n):
            total = block(dests[n], core)
            sibs[n].wait_recv()
            total = total + sib_in[r * NZ + n].astype(F32)
            if n < 2:
                line_out[r * NZ + n] = total.astype(BF16)
                send_line(n, beside)
            else:
                res[r, n - 2] = total

        def relay(r=r, line=line, send_line=send_line):
            line[0].wait_recv()
            line_out[r * NZ + 2] = (res[r, 0] + line_in[r * NZ].astype(F32)).astype(BF16)
            send_line(2, opposite)

        give(0)
        give(1)
        pass_on(0)
        give(2)
        pass_on(1)
        give(3)
        pass_on(2)
        if r == 1:
            relay()
        pass_on(3)
        finals.append((sibs, line, relay))
        if r == 0:
            continue
        page_at = lax.broadcasted_iota(jnp.int32, dpage_ref.shape, 1)
        page_of = lax.broadcasted_iota(jnp.int32, dpage_ref.shape, 0)
        for s in range(2):
            chosen = dpage_ref[...] == p * 2 + s
            owner = jnp.minimum(jnp.sum(jnp.where(chosen, page_at, 0)), NY * NX * NH - 1)
            side = jnp.where(jnp.sum(jnp.where(chosen, page_of, 0)) == full, 0, 1)
            for kv in range(2):
                dec_ref[s, 0, kv] = news[side, kv, owner // (NX * NH), (owner // NH) % NX, owner % NH]

    for ph in phases:
        for copies in ph.values():
            for one in copies:
                one.wait_send()
    for one in across:
        one.wait_send()
    for r in range(2):
        sibs, line, _ = finals[r]
        arrived(line[1:])
        res[r, 1] = res[r, 1] + line_in[r * NZ + 1].astype(F32) + line_in[r * NZ + 2].astype(F32)
    out_ref[0] = res[full, 1].astype(BF16)
    out_ref[1] = res[1 - full, 1].astype(BF16)

    for sibs, line, _ in finals:
        for one in sibs + line:
            one.wait_send()


def shards(queries, new_kv, kv_pool, block_owner, block_slot, prefix_len, decode_page, out_weight):
    vmem = pl.BlockSpec(memory_space=pltpu.VMEM)
    any_space = pl.BlockSpec(memory_space=pl.ANY)
    out, dec = pl.pallas_call(
        body,
        out_shape=(
            jax.ShapeDtypeStruct((2, PAGE, 512), BF16),
            jax.ShapeDtypeStruct((2, 1, 2, PAGE, HD), BF16),
        ),
        in_specs=[pl.BlockSpec(memory_space=pltpu.SMEM)] + [vmem] * 3 + [any_space] + [vmem] * 2 + [any_space],
        out_specs=(vmem, vmem),
        scratch_shapes=[
            pltpu.VMEM((2, NY, NX, 2, PAGE, HD), BF16),
            pltpu.VMEM((2, NY, NX, 2, PAGE, HD), BF16),
            pltpu.VMEM((2, 2, NY, NX, NH, PAGE, HD), BF16),
            pltpu.VMEM((2, PAGE, GROUP * HD), BF16),
            pltpu.VMEM((2, ROWS, HD), BF16),
            pltpu.VMEM((2, KB, HALF), F32),
            pltpu.VMEM((2, HD, ROWS), F32),
            pltpu.VMEM((2, 8, ROWS), F32),
            pltpu.VMEM((2, 8, ROWS), F32),
            pltpu.VMEM((GROUP * HD, 4096), BF16),
            pltpu.VMEM((PAGE, GROUP * HD), BF16),
            pltpu.VMEM((2 * NZ, PAGE, 512), BF16),
            pltpu.VMEM((2 * NZ, PAGE, 512), BF16),
            pltpu.VMEM((2 * NZ, PAGE, 512), BF16),
            pltpu.VMEM((2 * NZ, PAGE, 512), BF16),
            pltpu.VMEM((2, 2, PAGE, 512), F32),
            pltpu.VMEM((8, 128), jnp.int32),
            pltpu.SMEM((8, 128), jnp.int32),
            pltpu.SemaphoreType.DMA((160,)),
            pltpu.SemaphoreType.DMA((160,)),
            pltpu.SemaphoreType.DMA((3,)),
            pltpu.SemaphoreType.DMA((3,)),
            pltpu.SemaphoreType.DMA((8,)),
            pltpu.SemaphoreType.DMA((8,)),
            pltpu.SemaphoreType.DMA((8,)),
            pltpu.SemaphoreType.DMA((8,)),
            pltpu.SemaphoreType.DMA,
            pltpu.SemaphoreType.DMA,
            pltpu.SemaphoreType.DMA,
        ],
        compiler_params=pltpu.CompilerParams(
            collective_id=0, has_side_effects=True, vmem_limit_bytes=56 << 20
        ),
        cost_estimate=pl.CostEstimate(flops=11 * 10**9, bytes_accessed=10 << 20, transcendentals=16 << 20),
        name="paged_prefill",
    )(prefix_len, block_owner, block_slot, decode_page, queries, new_kv, kv_pool, out_weight)
    return out, dec


def solution(mesh):
    return jax.shard_map(
        shards,
        mesh=mesh,
        in_specs=(
            P(None, "pool", "tp"),
            P(None, "tp", None, "pool", None),
            P("pool", "tp", None, None, None),
            P(),
            P(),
            P(),
            P(),
            P("tp", None),
        ),
        out_specs=(P(None, "pool", "tp"), P("pool", "tp", None, None, None)),
        check_vma=False,
    )
```
